256 devices in a mesh: leaf: 256 (over y, x, z, core).
Axes of the slice: x: 4, y: 4, z: 8, core: 2. Of those that a mesh axis runs over, the one named last changes fastest.
Arguments:
- points: float32 [32, 262144], P(None, 'leaf'), may hold values from -6 to 6
- charges: float32 [32, 262144], P(None, 'leaf'), may hold values from -6 to 6
- leaf_skeleton: int32 [256, 256], P('leaf'), may hold values from 0 to 1023, as said below
- upper_skeleton: int32 [256, 3, 256], P('leaf'), may hold values from 0 to 511, as said below
- leaf_projection: float32 [256, 256, 1024], P('leaf'), as said below
- upper_projection: float32 [256, 3, 256, 512], P('leaf'), as said below
- near_leaves: int32 [256, 7], P('leaf'), may hold values from 0 to 255, as said below
- far_codes: int32 [256, 4, 2], P('leaf'), may hold values from 1 to 3, as said below
- regularizer: float32 [32], replicated, may hold values from 0.5 to 2
Outputs:
- potential: float32 [32, 262144], P(None, 'leaf')
The draws below stay inside these ranges and needn't reach their ends.
Inputs may be any that keep to these rules, and one draw needn't show every extreme that they name: `leaf_skeleton`: each row holds 256 distinct increasing indices of points within its leaf. `upper_skeleton`: entry [i, k] holds 256 distinct increasing indices into the 512 candidate skeleton points of the level k+1 node that holds leaf i, and is equal for all leaves of that node. `leaf_projection`: row r of leaf i's matrix is 1 in column leaf_skeleton[i, r] and 0 in the other skeleton columns. `upper_projection`: row r of entry [i, k] is 1 in column upper_skeleton[i, k, r] and 0 in the other skeleton columns; the entry is equal for all leaves of the level k+1 node that holds leaf i. `near_leaves`: row i holds 7 distinct leaves: i itself first, then leaves within 6 of i. `far_codes`: entry [i, k] holds two distinct increasing codes for the level k node that holds leaf i, equal for all leaves of that node.
All inputs are finite; a program needn't handle non-finite values.
Results may differ from the reference program's by a relative error of at most 0.0003.
Values sent between devices are 32-bit elements; how exact they have to be, the bound alone decides.
No kernel may reach another device: no remote copies, remote signals or barrier semaphores. Data moves between devices by JAX's collectives and lax.ppermute only.
A program may use at most 64 MiB of HBM per device.

```python
import math
import jax
import jax.numpy as jnp
from jax import lax

LEAF = 1024
DIM = 32
RHS = 32
RANK = 256
LEVELS = 4
NEAR_SPAN = 6
NEAR = 7
FAR = 2
POINTS = 262144
N_LEAF = 256


def leaf_skeleton_rows(key):
    key = jax.random.fold_in(key, 11)
    row_keys = jax.random.split(key, N_LEAF)

    def one_row(row_key):
        return jnp.sort(jax.random.permutation(row_key, LEAF)[:RANK])
    return jax.vmap(one_row)(row_keys).astype(jnp.int32)


def upper_skeleton_rows(key):
    key = jax.random.fold_in(key, 12)
    row_keys = jax.random.split(key, (LEVELS - 1) * N_LEAF)

    def one_row(row_key):
        return jnp.sort(jax.random.permutation(row_key, 2 * RANK)[:RANK])
    return jax.vmap(one_row)(row_keys).reshape(LEVELS - 1, N_LEAF, RANK).astype(jnp.int32)


def interpolation(skeleton, noise, columns):
    marks = skeleton[:, :, None] == jnp.arange(columns, dtype=jnp.int32)[None, None, :]
    taken = jnp.sum(marks.astype(jnp.int32), axis=1) > 0
    return jnp.where(taken[:, None, :], marks.astype(jnp.float32), noise)


def draw_leaf_skeleton(key, part):
    return leaf_skeleton_rows(key)


def draw_upper_skeleton(key, part):
    skeleton_rows = upper_skeleton_rows(key)
    leaves = jnp.arange(N_LEAF, dtype=jnp.int32)
    picked = [skeleton_rows[height - 1, jnp.right_shift(leaves, height)] for height in range(1, LEVELS)]
    return jnp.stack(picked, axis=1).astype(jnp.int32)


def draw_leaf_projection(key, part):
    skeleton = leaf_skeleton_rows(key)
    key = jax.random.fold_in(key, 15)
    scale = (LEAF - RANK) ** (-0.5)
    noise = jnp.clip(jax.random.normal(key, (N_LEAF, RANK, LEAF), jnp.float32), -4.0, 4.0) * scale
    return interpolation(skeleton, noise, LEAF).astype(jnp.float32)


def draw_upper_projection(key, part):
    skeleton_rows = upper_skeleton_rows(key)
    key = jax.random.fold_in(key, 16)
    scale = RANK ** (-0.5)
    leaves = jnp.arange(N_LEAF, dtype=jnp.int32)
    picked = []
    for height in range(1, LEVELS):
        level_key = jax.random.fold_in(key, height)
        nodes = N_LEAF >> height
        noise = jnp.clip(jax.random.normal(level_key, (nodes, RANK, 2 * RANK), jnp.float32), -4.0, 4.0) * scale
        matrices = interpolation(skeleton_rows[height - 1, :nodes], noise, 2 * RANK)
        picked.append(matrices[jnp.right_shift(leaves, height)])
    return jnp.stack(picked, axis=1).astype(jnp.float32)


def draw_near_leaves(key, part):
    key = jax.random.fold_in(key, 13)
    offsets = jnp.concatenate([jnp.arange(-NEAR_SPAN, 0), jnp.arange(1, NEAR_SPAN + 1)]).astype(jnp.int32)
    leaves = jnp.arange(N_LEAF, dtype=jnp.int32)[:, None]
    target = leaves + offsets[None, :]
    inside = (target >= 0) & (target < N_LEAF)
    scores = jax.random.randint(key, (N_LEAF, 2 * NEAR_SPAN), 0, 1 << 20)
    scores = jnp.where(inside, scores, 1 << 21) * (2 * NEAR_SPAN) + jnp.arange(2 * NEAR_SPAN, dtype=jnp.int32)[None, :]
    ranking = jnp.argsort(scores, axis=1)[:, :NEAR - 1]
    chosen = jnp.take_along_axis(target, ranking, axis=1)
    return jnp.concatenate([leaves, chosen], axis=1).astype(jnp.int32)


def draw_far_codes(key, part):
    key = jax.random.fold_in(key, 14)
    excluded = jax.random.randint(key, (LEVELS, N_LEAF), 1, 4)
    leaves = jnp.arange(N_LEAF, dtype=jnp.int32)
    picked = []
    for height in range(LEVELS):
        dropped = excluded[height, jnp.right_shift(leaves, height)]
        first_code = jnp.where(dropped == 1, 2, 1)
        second = jnp.where(dropped == 3, 2, 3)
        picked.append(jnp.stack([first_code, second], axis=1))
    return jnp.stack(picked, axis=1).astype(jnp.int32)


def steps_of(stream_key, shape, cuts, low, largest):
    factor_of = 1.0
    for dim, shards_of in cuts:
        steps = jax.random.uniform(jax.random.fold_in(jax.random.fold_in(stream_key, 6), dim), (shards_of,), jnp.float32, low / len(cuts), largest / len(cuts))
        factor_of = factor_of * jnp.repeat(jnp.exp(steps), shape[dim] // shards_of).reshape((-1,) + (1,) * (len(shape) - 1 - dim))
    return factor_of


def normal_values(key, dims, width, most, shards=(), kind=jnp.bfloat16):
    gain = steps_of(key, dims, shards, -0.22, 0.18) if shards else 1.0
    drawn = jax.random.normal(key, dims, jnp.float32) * width * gain
    return jnp.minimum(jnp.maximum(drawn, -most), most).astype(kind)


def setup_inputs(seed: int = 0) -> dict:
    streams_of = jax.random.split(jax.random.key(seed), 10)
    return {
        "points": normal_values(streams_of[0], (DIM, POINTS), 1.0, 6.0, ((1, 256),), jnp.float32),
        "charges": normal_values(streams_of[1], (RHS, POINTS), 1.0, 6.0, ((1, 256),), jnp.float32),
        "leaf_skeleton": draw_leaf_skeleton(jax.random.fold_in(streams_of[9], 71), 0),
        "upper_skeleton": draw_upper_skeleton(jax.random.fold_in(streams_of[9], 71), 0),
        "leaf_projection": draw_leaf_projection(jax.random.fold_in(streams_of[9], 71), 0),
        "upper_projection": draw_upper_projection(jax.random.fold_in(streams_of[9], 71), 0),
        "near_leaves": draw_near_leaves(jax.random.fold_in(streams_of[9], 71), 0),
        "far_codes": draw_far_codes(jax.random.fold_in(streams_of[9], 71), 0),
        "regularizer": jnp.clip(jnp.exp(jax.random.uniform(streams_of[8], (RHS,), jnp.float32, math.log(0.5), math.log(2.0))), 0.5, 2.0),
    }


inverse_width = 1.0 / 16.0


def kernel(left_set, right_set):
    cross = lax.dot_general(left_set, right_set, (((0,), (0,)), ((), ())), precision=lax.Precision.HIGHEST, preferred_element_type=jnp.float32)
    distance = jnp.sum(left_set * left_set, axis=0)[:, None] + jnp.sum(right_set * right_set, axis=0)[None, :] - 2.0 * cross
    return jnp.exp(-inverse_width * distance)


def apply_rows(weights, kernel_tile):
    return lax.dot_general(weights, kernel_tile, (((1,), (1,)), ((), ())), precision=lax.Precision.HIGHEST, preferred_element_type=jnp.float32)


def spread(weights, kernel_tile):
    return jnp.dot(weights, kernel_tile, precision=lax.Precision.HIGHEST, preferred_element_type=jnp.float32)


def take_columns(source, chosen):
    return jnp.take(source, chosen, axis=1)


def far_term(own_points, other_points, other_weights):
    return apply_rows(other_weights, kernel(own_points, other_points))


def reference(points, charges, leaf_skeleton, upper_skeleton, leaf_projection, upper_projection, near_leaves, far_codes, regularizer):
    leaves = N_LEAF
    leaf_points = points.reshape(DIM, leaves, LEAF).transpose(1, 0, 2)
    leaf_charges = charges.reshape(RHS, leaves, LEAF).transpose(1, 0, 2)
    node_points = jax.vmap(take_columns)(leaf_points, leaf_skeleton)
    node_weights = jax.vmap(apply_rows)(leaf_charges, leaf_projection)
    far_list = []
    tiles = []
    for height in range(LEVELS):
        node_count = leaves >> height
        nodes = jnp.arange(node_count, dtype=jnp.int32)
        codes = far_codes[nodes << height, height]
        accum = jnp.zeros((node_count, RHS, RANK), jnp.float32)
        for position in range(FAR):
            partner = jnp.bitwise_xor(nodes, codes[:, position])
            accum = accum + jax.vmap(far_term)(node_points, node_points[partner], node_weights[partner])
        far_list.append(accum)
        if height + 1 < LEVELS:
            parents = node_count // 2
            cand_points = node_points.reshape(parents, 2, DIM, RANK).transpose(0, 2, 1, 3).reshape(parents, DIM, 2 * RANK)
            cand_weights = node_weights.reshape(parents, 2, RHS, RANK).transpose(0, 2, 1, 3).reshape(parents, RHS, 2 * RANK)
            parent_rows = jnp.arange(parents, dtype=jnp.int32) << (height + 1)
            chosen = upper_skeleton[parent_rows, height]
            projections = upper_projection[parent_rows, height]
            node_points = jax.vmap(take_columns)(cand_points, chosen)
            node_weights = jax.vmap(apply_rows)(cand_weights, projections)
            tiles.append(projections)
    local_field = far_list[LEVELS - 1]
    for height in reversed(range(LEVELS - 1)):
        down_field = jax.vmap(spread)(local_field, tiles[height])
        parents = down_field.shape[0]
        down_field = down_field.reshape(parents, RHS, 2, RANK).transpose(0, 2, 1, 3).reshape(parents * 2, RHS, RANK)
        local_field = far_list[height] + down_field
    far_out = jax.vmap(spread)(local_field, leaf_projection)
    zero_index = jnp.zeros((), jnp.int32)

    def near_block(leaf_index):
        own_points = lax.dynamic_slice(points, (zero_index, leaf_index * LEAF), (DIM, LEAF))
        accum = jnp.zeros((RHS, LEAF), jnp.float32)
        for position in range(NEAR):
            other = near_leaves[leaf_index, position].astype(jnp.int32)
            other_points = lax.dynamic_slice(points, (zero_index, other * LEAF), (DIM, LEAF))
            other_charges = lax.dynamic_slice(charges, (zero_index, other * LEAF), (RHS, LEAF))
            accum = accum + apply_rows(other_charges, kernel(own_points, other_points))
        return accum

    near_out = lax.map(near_block, jnp.arange(leaves, dtype=jnp.int32))
    result = (far_out + near_out) + regularizer[None, :, None] * leaf_charges
    return result.transpose(1, 0, 2).reshape(RHS, leaves * LEAF)
```

```python
import functools
import math
import jax
import jax.numpy as jnp
from jax import lax
from jax.experimental import pallas as pl
from jax.experimental.pallas import tpu as pltpu
from jax.sharding import PartitionSpec as P

RANK = 256
LEVELS = 4
BLOCK = 256

f32 = jnp.float32
bf16 = jnp.bfloat16
SCALE = math.log2(math.e) / 16.0
NN = (((1,), (0,)), ((), ()))
NT = (((1,), (1,)), ((), ()))
VMEM = pl.BlockSpec(memory_space=pltpu.VMEM)
ANY = pl.BlockSpec(memory_space=pl.ANY)
HBM = pl.BlockSpec(memory_space=pltpu.HBM)


def mm(left, right, dims=NN):
    return lax.dot_general(left, right, dims, preferred_element_type=f32)


def split2(value):
    high = value.astype(bf16)
    return high, (value - high.astype(f32)).astype(bf16)


def split3(value):
    high = value.astype(bf16)
    rest = value - high.astype(f32)
    middle = rest.astype(bf16)
    return high, middle, (rest - middle.astype(f32)).astype(bf16)


def stack3(value):
    return jnp.concatenate(split3(value), axis=0)


def sum3(value):
    rows = value.shape[0] // 3
    return value[:rows] + value[rows : 2 * rows] + value[2 * rows :]


def norm_rows(value, first):
    count = value.shape[1]
    parts = split3(-SCALE * jnp.sum(value * value, axis=0, keepdims=True))
    parts = [part.astype(f32) for part in parts]
    ones = jnp.ones((3, count), f32)
    pad = jnp.zeros((10, count), f32)
    order = [*parts, ones, pad] if first else [ones, *parts, pad]
    return jnp.concatenate(order, axis=0).astype(bf16)


def own_features(points):
    a, b, c = split3(points * (2.0 * SCALE))
    return jnp.concatenate([a, a, b, b, a, c, norm_rows(points, True)], axis=0)


def other_features(points):
    a, b, c = split3(points)
    return jnp.concatenate([a, b, a, b, c, a, norm_rows(points, False)], axis=0)


def kernel_pieces(other, own):
    return split2(jnp.exp2(mm(other, own)))


def add_tile(other_points, other_charges, feature_ref, total_ref):
    other = other_features(other_points).T
    weights = stack3(other_charges)
    size = feature_ref.shape[1]
    for column in range(0, size, BLOCK):
        own = feature_ref[:, column : column + BLOCK]
        total = total_ref[:, column : column + BLOCK]
        for row in range(0, size, BLOCK):
            high, low = kernel_pieces(other[row : row + BLOCK], own)
            part = weights[:, row : row + BLOCK]
            total = total + mm(part, high) + mm(part, low)
        total_ref[:, column : column + BLOCK] = total


def pair(points, charges, other_points, other_charges, out):
    half = points.shape[0]
    for place, part in enumerate((points, charges, other_points, other_charges)):
        out[half * place : half * (place + 1)] = part[...]


def leaf_node(chip, chosen, matrix, out):
    size = chip.shape[1]
    spots = lax.broadcasted_iota(jnp.int32, (size, RANK), 0)
    marks = (spots == chosen[...]).astype(f32).astype(bf16)
    out[:32] = sum3(mm(stack3(chip[:32]), marks))
    high, low = split2(matrix[0])
    weights = stack3(chip[32:64])
    out[32:] = sum3(mm(weights, high, NT) + mm(weights, low, NT))


def near_first(near, chip, token, near_out, features, total):
    size = total.shape[1]
    me = lax.axis_index("leaf")
    features[...] = own_features(chip[:32])
    total[...] = jnp.zeros_like(total)
    add_tile(chip[:32], chip[32:64], features, total)
    sibling = me + 1 - 2 * lax.rem(me, 2)
    wanted = jnp.sum((near[...] == sibling).astype(jnp.int32))

    @pl.when(wanted > 0)
    def _():
        add_tile(chip[64:96], chip[96:], features, total)

    near_out[...] = sum3(total[...])


def near_blocks(entries, count, near, near_in, features, token, *refs):
    sources = refs[:count]
    near_out, slots, total, sems = refs[count:]
    me = lax.axis_index("leaf")
    sign = 2 * lax.rem(me, 2) - 1
    wanted = jnp.sum(lax.shift_left(jnp.int32(1), near[...] - me + 6))
    taken = jnp.int32(0)
    for source, row, offset in entries:
        bit = lax.rem(lax.shift_right_logical(wanted, sign * offset + 6), 2)

        @pl.when(bit == 1)
        def _(source=source, row=row, slot=taken):
            pltpu.make_async_copy(
                sources[source].at[pl.ds(row, 64)], slots.at[slot], sems.at[slot]
            ).start()

        taken = taken + bit
    total[...] = jnp.zeros_like(total)

    def step(slot, carry):
        pltpu.make_async_copy(
            sources[0].at[pl.ds(0, 64)], slots.at[slot], sems.at[slot]
        ).wait()
        add_tile(slots[slot, :32], slots[slot, 32:], features, total)
        return carry

    lax.fori_loop(0, taken, step, 0)
    near_out[...] = near_in[...] + sum3(total[...])


def merge(level, own, sibling, chosen, matrix, token, sent, extra=None):
    me = lax.axis_index("leaf")
    right = lax.rem(lax.shift_right_logical(me, level), 2)
    kind = lax.rem(me, 2)
    if level == 0:
        rows = pl.ds(pl.multiple_of(kind * 32, 32), 32)
        mine = own[rows, :]
        theirs = sibling[rows, :]
    else:
        mine = own[:, 2 * RANK :]
        theirs = sibling[:, 2 * RANK :]
        extra[:, : 2 * RANK] = sibling[:, : 2 * RANK]
        extra[:, 2 * RANK : 3 * RANK] = mine
        extra[:, 3 * RANK :] = theirs
    sent[:, :RANK] = mine
    sent[:, RANK : 2 * RANK] = theirs
    if level == LEVELS - 1:
        return
    mine = stack3(mine)
    theirs = stack3(theirs)
    first = right * RANK
    second = RANK - first

    @pl.when(kind == 0)
    def _():
        spots = lax.broadcasted_iota(jnp.int32, (RANK, RANK), 0)
        row = chosen[level]
        left_marks = (spots + first == row).astype(f32).astype(bf16)
        right_marks = (spots + second == row).astype(f32).astype(bf16)
        sent[:, 2 * RANK :] = sum3(mm(mine, left_marks) + mm(theirs, right_marks))

    @pl.when(kind == 1)
    def _():
        near_high, near_low = split2(
            matrix[0, level, :, pl.ds(pl.multiple_of(first, RANK), RANK)]
        )
        far_high, far_low = split2(
            matrix[0, level, :, pl.ds(pl.multiple_of(second, RANK), RANK)]
        )
        sent[:, 2 * RANK :] = sum3(
            (mm(mine, near_high, NT) + mm(mine, near_low, NT))
            + (mm(theirs, far_high, NT) + mm(theirs, far_low, NT))
        )


def sorted_kinds(pair, mine, theirs):
    kind = lax.rem(lax.axis_index("leaf"), 2)
    left = pair[0][:, RANK * mine : RANK * (mine + 1)]
    right = pair[1][:, RANK * theirs : RANK * (theirs + 1)]
    return jnp.where(kind == 0, left, right), jnp.where(kind == 0, right, left)


def far_level(level, codes, own, choices):
    picked = []
    for position in range(2):
        code = codes[0, position : position + 1, level : level + 1]
        picked.append(
            [
                jnp.where(code == 1, one, jnp.where(code == 2, two, three))
                for one, two, three in zip(*choices, strict=True)
            ]
        )
    others = jnp.concatenate([picked[0][0], picked[1][0]], axis=1)
    weights = stack3(jnp.concatenate([picked[0][1], picked[1][1]], axis=1))
    high, low = kernel_pieces(other_features(others).T, own_features(own))
    return sum3(mm(weights, high) + mm(weights, low))


def far_lower(codes, leaf_own, leaf_sibling, *refs):
    kept = [refs[0:2], refs[2:4], refs[4:6]]
    out = refs[6]
    choices = [
        (leaf_sibling[:32], leaf_sibling[32:]),
        sorted_kinds(kept[0], 0, 1),
        sorted_kinds(kept[0], 1, 0),
    ]
    out[:32] = far_level(0, codes, leaf_own[:32], choices)
    for level in (1, 2):
        choices = [
            sorted_kinds(kept[level - 1], 3, 3),
            sorted_kinds(kept[level], 0, 0),
            sorted_kinds(kept[level], 1, 1),
        ]
        own = sorted_kinds(kept[level - 1], 2, 2)[0]
        out[32 * level : 32 * level + 32] = far_level(level, codes, own, choices)


def finish(
    codes, gain, chip, leaf_matrix, upper_matrix, near_field, lower, kept, kept_other, last, last_other, out
):
    me = lax.axis_index("leaf")
    kept = (kept, kept_other)
    last = (last, last_other)
    choices = [sorted_kinds(kept, 3, 3), sorted_kinds(last, 0, 0), sorted_kinds(last, 1, 1)]
    local = far_level(3, codes, sorted_kinds(kept, 2, 2)[0], choices)
    for level in reversed(range(LEVELS - 1)):
        right = lax.rem(lax.shift_right_logical(me, level), 2)
        columns = pl.ds(pl.multiple_of(right * RANK, RANK), RANK)
        half = upper_matrix[0, level, :, columns]
        high, low = split2(half)
        pieces = stack3(local)
        local = lower[32 * level : 32 * level + 32] + sum3(mm(pieces, high) + mm(pieces, low))
    high, low = split2(leaf_matrix[0])
    pieces = stack3(local)
    far_out = sum3(mm(pieces, high) + mm(pieces, low))
    count = gain.shape[1]
    diagonal = lax.broadcasted_iota(jnp.int32, (count, count), 0) == lax.broadcasted_iota(
        jnp.int32, (count, count), 1
    )
    column = jnp.sum(jnp.where(diagonal, gain[...], 0.0), axis=1, keepdims=True)
    out[...] = far_out + near_field[...] + column * chip[32:64]


def call(function, shapes, in_specs, flops, scratch=(), limit=16, **extra):
    many = isinstance(shapes, list)
    return pl.pallas_call(
        function,
        out_shape=shapes,
        in_specs=in_specs,
        out_specs=[VMEM] * len(shapes) if many else VMEM,
        scratch_shapes=list(scratch),
        cost_estimate=pl.CostEstimate(flops=flops, bytes_accessed=1 << 20, transcendentals=0),
        compiler_params=pltpu.CompilerParams(vmem_limit_bytes=limit << 20),
        **extra,
    )


def gate(value, token, out):
    pass


def after(value, token):
    return pl.pallas_call(
        gate,
        out_shape=shape(*value.shape),
        in_specs=[ANY, ANY],
        out_specs=ANY,
        input_output_aliases={0: 0},
        compiler_params=pltpu.CompilerParams(vmem_limit_bytes=1 << 20),
    )(value, token)


def shape(rows, columns, kind=f32):
    return jax.ShapeDtypeStruct((rows, columns), kind)


def body(
    points,
    charges,
    leaf_skeleton,
    upper_skeleton,
    leaf_projection,
    upper_projection,
    near_leaves,
    far_codes,
    regularizer,
):
    devices = lax.axis_size("leaf")
    size = points.shape[1]

    def partner(value, bit):
        return lax.ppermute(value, "leaf", [(leaf, leaf ^ (1 << bit)) for leaf in range(devices)])

    def along(value, chips):
        pairs = [(leaf, leaf + 2 * chips * (1 - 2 * (leaf % 2))) for leaf in range(devices)]
        pairs = [(source, target) for source, target in pairs if 0 <= target < devices]
        return lax.ppermute(value, "leaf", pairs)

    def near_step(near_field, token, sources, entries):
        count = len(sources)
        return call(
            functools.partial(near_blocks, entries, count),
            shape(32, size),
            [VMEM] * 3 + [ANY] * (1 + count),
            4 * 10**10,
            [
                pltpu.VMEM((len(entries), 64, size), f32),
                pltpu.VMEM((96, size), f32),
                pltpu.SemaphoreType.DMA((len(entries),)),
            ],
        )(near_leaves, near_field, features, token, *sources)

    def merge_step(level, own, sibling, token):
        shapes = [shape(32, (3 if level < LEVELS - 1 else 2) * RANK)]
        if level > 0:
            shapes.append(shape(32, 4 * RANK))
        return call(functools.partial(merge, level), shapes, [VMEM] * 4 + [ANY], 10**8)(
            own, sibling, upper_chosen, upper_projection, token
        )

    upper_chosen = jnp.transpose(upper_skeleton, (1, 0, 2))
    codes = jnp.transpose(far_codes, (0, 2, 1))

    chip = call(pair, shape(128, size), [VMEM] * 4, 10**8)(
        points, charges, partner(points, 0), partner(charges, 0)
    )
    got2 = along(chip, 2)
    got1 = along(chip, 1)
    node = call(leaf_node, shape(64, RANK), [VMEM] * 3, 10**11)(
        chip, leaf_skeleton, leaf_projection
    )
    sibling_node = partner(node, 0)
    (sent1,) = merge_step(0, node, sibling_node, node)
    far1 = partner(sent1, 1)
    near_field, features = call(
        near_first,
        [shape(32, size), shape(208, size, bf16)],
        [VMEM] * 2 + [ANY],
        2 * 10**9,
        [pltpu.VMEM((96, size), f32)],
    )(near_leaves, chip, sent1)
    got2 = after(got2, near_field)
    sent2, kept2 = merge_step(1, sent1, far1, got2)
    far2 = partner(sent2, 2)
    kept2_other = partner(kept2, 0)
    got3 = along(got2, 1)
    other2 = partner(got2, 0)
    sent3, kept3 = merge_step(2, sent2, far2, near_field)
    far3 = partner(sent3, 3)
    kept3_other = partner(kept3, 0)
    got1 = after(got1, sent2)
    other1 = partner(got1, 0)
    entries = [(0, 0, 4), (0, 64, 3), (1, 0, -5), (1, 64, -4)]
    entries += [(2, 0, 2), (2, 64, 1), (3, 0, -3), (3, 64, -2)]
    near_field = near_step(near_field, sent3, [got2, other2, got1, other1], entries)
    sent4, kept4 = merge_step(3, sent3, far3, near_field)
    far4 = partner(sent4, 4)
    kept4_other = partner(kept4, 0)
    got3 = after(got3, near_field)
    other3 = partner(got3, 0)
    lower = call(far_lower, shape(96, RANK), [VMEM] * 9, 10**10)(
        codes, node, sibling_node, kept2, kept2_other, kept3, kept3_other, kept4, kept4_other
    )
    far4_other = partner(after(far4, lower), 0)
    entries = [(0, 0, 6), (0, 64, 5), (1, 64, -6)]
    near_field = near_step(near_field, lower, [got3, other3], entries)
    return call(finish, shape(32, size), [VMEM] * 11, 10**9)(
        codes,
        regularizer[None, :],
        chip,
        leaf_projection,
        upper_projection,
        near_field,
        lower,
        kept4,
        kept4_other,
        far4,
        far4_other,
    )


def solution(mesh):
    placed = (
        P(None, "leaf"),
        P(None, "leaf"),
        P("leaf", None),
        P("leaf", None, None),
        P("leaf", None, None),
        P("leaf", None, None, None),
        P("leaf", None),
        P("leaf", None, None),
        P(),
    )
    return jax.shard_map(
        body, mesh=mesh, in_specs=placed, out_specs=P(None, "leaf"), check_vma=False
    )
```

```python
import functools
import math
import jax
import jax.numpy as jnp
from jax import lax
from jax.experimental import pallas as pl
from jax.experimental.pallas import tpu as pltpu
from jax.sharding import PartitionSpec as P

RANK = 256
LEVELS = 4
BLOCK = 256

f32 = jnp.float32
bf16 = jnp.bfloat16
SCALE = math.log2(math.e) / 16.0
NN = (((1,), (0,)), ((), ()))
NT = (((1,), (1,)), ((), ()))
VMEM = pl.BlockSpec(memory_space=pltpu.VMEM)
ANY = pl.BlockSpec(memory_space=pl.ANY)
HBM = pl.BlockSpec(memory_space=pltpu.HBM)


def mm(left, right, dims=NN):
    return lax.dot_general(left, right, dims, preferred_element_type=f32)


def split2(value):
    high = value.astype(bf16)
    return high, (value - high.astype(f32)).astype(bf16)


def split3(value):
    high = value.astype(bf16)
    rest = value - high.astype(f32)
    middle = rest.astype(bf16)
    return high, middle, (rest - middle.astype(f32)).astype(bf16)


def stack3(value):
    return jnp.concatenate(split3(value), axis=0)


def sum3(value):
    rows = value.shape[0] // 3
    return value[:rows] + value[rows : 2 * rows] + value[2 * rows :]


def norm_rows(value, first):
    count = value.shape[1]
    parts = split3(-SCALE * jnp.sum(value * value, axis=0, keepdims=True))
    parts = [part.astype(f32) for part in parts]
    ones = jnp.ones((3, count), f32)
    pad = jnp.zeros((10, count), f32)
    order = [*parts, ones, pad] if first else [ones, *parts, pad]
    return jnp.concatenate(order, axis=0).astype(bf16)


def own_features(points):
    a, b, c = split3(points * (2.0 * SCALE))
    return jnp.concatenate([a, a, b, b, a, c, norm_rows(points, True)], axis=0)


def other_features(points):
    a, b, c = split3(points)
    return jnp.concatenate([a, b, a, b, c, a, norm_rows(points, False)], axis=0)


def kernel_pieces(other, own):
    return split2(jnp.exp2(mm(other, own)))


def add_tile(other_points, other_charges, feature_ref, total_ref):
    other = other_features(other_points).T
    weights = stack3(other_charges)
    size = feature_ref.shape[1]
    for column in range(0, size, BLOCK):
        own = feature_ref[:, column : column + BLOCK]
        total = total_ref[:, column : column + BLOCK]
        for row in range(0, size, BLOCK):
            high, low = kernel_pieces(other[row : row + BLOCK], own)
            part = weights[:, row : row + BLOCK]
            total = total + mm(part, high) + mm(part, low)
        total_ref[:, column : column + BLOCK] = total


def pair(points, charges, other_points, other_charges, out):
    half = points.shape[0]
    for place, part in enumerate((points, charges, other_points, other_charges)):
        out[half * place : half * (place + 1)] = part[...]


def leaf_node(chip, chosen, matrix, out):
    size = chip.shape[1]
    spots = lax.broadcasted_iota(jnp.int32, (size, RANK), 0)
    marks = (spots == chosen[...]).astype(f32).astype(bf16)
    out[:32] = sum3(mm(stack3(chip[:32]), marks))
    high, low = split2(matrix[0])
    weights = stack3(chip[32:64])
    out[32:] = sum3(mm(weights, high, NT) + mm(weights, low, NT))


def near_first(near, chip, token, near_out, features, total):
    size = total.shape[1]
    me = lax.axis_index("leaf")
    features[...] = own_features(chip[:32])
    total[...] = jnp.zeros_like(total)
    add_tile(chip[:32], chip[32:64], features, total)
    sibling = me + 1 - 2 * lax.rem(me, 2)
    wanted = jnp.sum((near[...] == sibling).astype(jnp.int32))

    @pl.when(wanted > 0)
    def _():
        add_tile(chip[64:96], chip[96:], features, total)

    near_out[...] = sum3(total[...])


def near_blocks(entries, count, near, near_in, features, token, *refs):
    sources = refs[:count]
    near_out, slots, total, sems = refs[count:]
    me = lax.axis_index("leaf")
    sign = 2 * lax.rem(me, 2) - 1
    wanted = jnp.sum(lax.shift_left(jnp.int32(1), near[...] - me + 6))
    taken = jnp.int32(0)
    for source, row, offset in entries:
        bit = lax.rem(lax.shift_right_logical(wanted, sign * offset + 6), 2)

        @pl.when(bit == 1)
        def _(source=source, row=row, slot=taken):
            pltpu.make_async_copy(
                sources[source].at[pl.ds(row, 64)], slots.at[slot], sems.at[slot]
            ).start()

        taken = taken + bit
    total[...] = jnp.zeros_like(total)

    def step(slot, carry):
        pltpu.make_async_copy(
            sources[0].at[pl.ds(0, 64)], slots.at[slot], sems.at[slot]
        ).wait()
        add_tile(slots[slot, :32], slots[slot, 32:], features, total)
        return carry

    lax.fori_loop(0, taken, step, 0)
    near_out[...] = near_in[...] + sum3(total[...])


def block_of(ref, place):
    return ref[:, RANK * place : RANK * (place + 1)]


def merge(level, own, sibling, chosen, matrix, token, sent, *more):
    me = lax.axis_index("leaf")
    right = lax.rem(lax.shift_right_logical(me, level), 2)
    kind = lax.rem(me, 2)
    if level == 0:
        rows = pl.ds(pl.multiple_of(kind * 32, 32), 32)
        mine = own[rows, :]
        theirs = sibling[rows, :]
    else:
        mine = block_of(own, 2)
        theirs = block_of(sibling, 2)
        kept = more[-1]
        kept[:, : 2 * RANK] = sibling[:, : 2 * RANK]
        kept[:, 2 * RANK : 3 * RANK] = mine
        kept[:, 3 * RANK : 4 * RANK] = theirs
    sent[:, :RANK] = mine
    sent[:, RANK : 2 * RANK] = theirs
    mine = stack3(mine)
    theirs = stack3(theirs)
    first = right * RANK
    second = RANK - first

    @pl.when(kind == 0)
    def _():
        spots = lax.broadcasted_iota(jnp.int32, (RANK, RANK), 0)
        left_marks = (spots + first == chosen[level]).astype(f32).astype(bf16)
        right_marks = (spots + second == chosen[level]).astype(f32).astype(bf16)
        sent[:, 2 * RANK :] = sum3(mm(mine, left_marks) + mm(theirs, right_marks))

    @pl.when(kind == 1)
    def _():
        near_high, near_low = split2(
            matrix[0, level, :, pl.ds(pl.multiple_of(first, RANK), RANK)]
        )
        far_high, far_low = split2(
            matrix[0, level, :, pl.ds(pl.multiple_of(second, RANK), RANK)]
        )
        sent[:, 2 * RANK :] = sum3(
            (mm(mine, near_high, NT) + mm(mine, near_low, NT))
            + (mm(theirs, far_high, NT) + mm(theirs, far_low, NT))
        )

    if level == 2:
        more[0][...] = block_of(sent, 2)
        kept[:, 4 * RANK :] = block_of(sent, 2)


def collect(far_one, far_two, far_three, token, out):
    out[:, : 3 * RANK] = far_one[...]
    out[:, 3 * RANK : 4 * RANK] = far_two[...]
    out[:, 4 * RANK :] = far_three[...]


def sorted_kinds(pair, mine, theirs):
    kind = lax.rem(lax.axis_index("leaf"), 2)
    left = block_of(pair[0], mine)
    right = block_of(pair[1], theirs)
    return jnp.where(kind == 0, left, right), jnp.where(kind == 0, right, left)


def far_level(level, codes, own, choices):
    picked = []
    for position in range(2):
        code = codes[0, position : position + 1, level : level + 1]
        picked.append(
            [
                jnp.where(code == 1, one, jnp.where(code == 2, two, three))
                for one, two, three in zip(*choices, strict=True)
            ]
        )
    others = jnp.concatenate([picked[0][0], picked[1][0]], axis=1)
    weights = stack3(jnp.concatenate([picked[0][1], picked[1][1]], axis=1))
    high, low = kernel_pieces(other_features(others).T, own_features(own))
    return sum3(mm(weights, high) + mm(weights, low))


def product(left, right):
    high, low = split2(right)
    pieces = stack3(left)
    return sum3(mm(pieces, high) + mm(pieces, low))


def half_of(matrix, level):
    right = lax.rem(lax.shift_right_logical(lax.axis_index("leaf"), level), 2)
    return matrix[0, level, :, pl.ds(pl.multiple_of(right * RANK, RANK), RANK)]


def compose(upper_matrix, leaf_matrix, token, out):
    value = leaf_matrix[0]
    for level in range(3):
        value = product(half_of(upper_matrix, level), value)
        out[level] = value


def far_first(
    codes, gain, mine, leaf_matrix, composed, leaf_own, leaf_sibling, low, low_other, middle, middle_other, token, out
):
    low = (low, low_other)
    middle = (middle, middle_other)
    choices = [
        (leaf_sibling[:32], leaf_sibling[32:]),
        sorted_kinds(low, 0, 1),
        sorted_kinds(low, 1, 0),
    ]
    first = far_level(0, codes, leaf_own[:32], choices)
    choices = [sorted_kinds(low, 3, 3), sorted_kinds(middle, 0, 0), sorted_kinds(middle, 1, 1)]
    second = far_level(1, codes, sorted_kinds(low, 2, 2)[0], choices)
    count = gain.shape[1]
    diagonal = lax.broadcasted_iota(jnp.int32, (count, count), 0) == lax.broadcasted_iota(
        jnp.int32, (count, count), 1
    )
    column = jnp.sum(jnp.where(diagonal, gain[...], 0.0), axis=1, keepdims=True)
    far_out = product(first, leaf_matrix[0]) + product(second, composed[0])
    out[...] = far_out + column * mine[32:64]


def finish(codes, composed, near_field, lower, kept, kept_other, last, last_other, out):
    kept = (kept, kept_other)
    last = (last, last_other)
    choices = [sorted_kinds(kept, 3, 3), sorted_kinds(last, 0, 0), sorted_kinds(last, 1, 1)]
    third = far_level(2, codes, sorted_kinds(kept, 2, 2)[0], choices)
    choices = [sorted_kinds(last, place, place) for place in (2, 3, 4)]
    fourth = far_level(3, codes, sorted_kinds(kept, 4, 4)[0], choices)
    far_out = product(third, composed[1]) + product(fourth, composed[2])
    out[...] = (far_out + lower[...]) + near_field[...]


def call(function, shapes, in_specs, flops, scratch=(), limit=16, **extra):
    many = isinstance(shapes, list)
    return pl.pallas_call(
        function,
        out_shape=shapes,
        in_specs=in_specs,
        out_specs=[VMEM] * len(shapes) if many else VMEM,
        scratch_shapes=list(scratch),
        cost_estimate=pl.CostEstimate(flops=flops, bytes_accessed=1 << 20, transcendentals=0),
        compiler_params=pltpu.CompilerParams(vmem_limit_bytes=limit << 20),
        **extra,
    )


def gate(value, token, out):
    pass


def halve(value, token, whole, upper, lower):
    whole[...] = value[...]
    upper[...] = value[:64]
    lower[...] = value[64:]


def second_half(value, token, out):
    out[...] = value[64:]


def after(value, token):
    return pl.pallas_call(
        gate,
        out_shape=shape(*value.shape),
        in_specs=[ANY, ANY],
        out_specs=ANY,
        input_output_aliases={0: 0},
        compiler_params=pltpu.CompilerParams(vmem_limit_bytes=1 << 20),
    )(value, token)


def shape(rows, columns, kind=f32):
    return jax.ShapeDtypeStruct((rows, columns), kind)


def body(
    points,
    charges,
    leaf_skeleton,
    upper_skeleton,
    leaf_projection,
    upper_projection,
    near_leaves,
    far_codes,
    regularizer,
):
    devices = lax.axis_size("leaf")
    size = points.shape[1]

    def partner(value, bit):
        return lax.ppermute(value, "leaf", [(leaf, leaf ^ bit) for leaf in range(devices)])

    def along(value, chips):
        pairs = [(leaf, leaf + 2 * chips * (1 - 2 * (leaf % 2))) for leaf in range(devices)]
        pairs = [(source, target) for source, target in pairs if 0 <= target < devices]
        return lax.ppermute(value, "leaf", pairs)

    def near_step(near_field, token, sources, entries, flops):
        count = len(sources)
        return call(
            functools.partial(near_blocks, entries, count),
            shape(32, size),
            [VMEM] * 3 + [ANY] * (1 + count),
            flops,
            [
                pltpu.VMEM((len(entries), 64, size), f32),
                pltpu.VMEM((96, size), f32),
                pltpu.SemaphoreType.DMA((len(entries),)),
            ],
        )(near_leaves, near_field, features, token, *sources)

    def merge_step(level, own, sibling, token):
        shapes = [shape(32, 3 * RANK)]
        if level == 1:
            shapes += [shape(32, 4 * RANK)]
        if level == 2:
            shapes += [shape(32, RANK), shape(32, 5 * RANK)]
        return call(functools.partial(merge, level), shapes, [VMEM] * 4 + [ANY], 10**8)(
            own, sibling, upper_chosen, upper_projection, token
        )

    upper_chosen = jnp.transpose(upper_skeleton, (1, 0, 2))
    codes = jnp.transpose(far_codes, (0, 2, 1))

    chip = call(pair, shape(128, size), [VMEM] * 4, 10**8)(
        points, charges, partner(points, 1), partner(charges, 1)
    )
    got2 = along(chip, 2)
    got1 = along(chip, 1)
    node = call(leaf_node, shape(64, RANK), [VMEM] * 3, 10**11)(
        chip, leaf_skeleton, leaf_projection
    )
    sibling_node = partner(node, 1)
    (sent1,) = merge_step(0, node, sibling_node, node)
    far1 = partner(sent1, 2)
    near_field, features = call(
        near_first,
        [shape(32, size), shape(208, size, bf16)],
        [VMEM] * 2 + [ANY],
        10**5,
        [pltpu.VMEM((96, size), f32)],
    )(near_leaves, chip, sent1)
    composed = call(
        compose,
        jax.ShapeDtypeStruct((3, RANK, size), f32),
        [VMEM, VMEM, ANY],
        10**5,
    )(upper_projection, leaf_projection, near_field)
    got2, upper2, lower2 = call(
        halve, [shape(128, size), shape(64, size), shape(64, size)], [VMEM, ANY], 10**5
    )(got2, composed)
    sources = [got2, partner(upper2, 1), partner(lower2, 1)]
    entries = [(0, 0, 4), (0, 64, 3), (1, 0, -5), (2, 0, -4)]
    near_field = near_step(near_field, composed, sources, entries, 10**5)
    sent2, kept2 = merge_step(1, sent1, far1, near_field)
    far2 = partner(sent2, 4)
    kept2_other = partner(kept2, 1)
    got1 = after(got1, sent2)
    got3 = along(got2, 1)
    other1 = partner(got1, 1)
    sent3, sent_few, kept3 = merge_step(2, sent2, far2, near_field)
    far_one = partner(sent3, 8)
    far_two = partner(sent_few, 16)
    far_three = partner(sent_few, 24)
    kept3_other = partner(kept3, 1)
    entries = [(0, 0, 2), (0, 64, 1), (1, 0, -3), (1, 64, -2)]
    near_field = near_step(near_field, sent3, [got1, other1], entries, 4 * 10**10)
    lower = call(far_first, shape(32, size), [VMEM] * 11 + [ANY], 10**8)(
        codes,
        regularizer[None, :],
        chip,
        leaf_projection,
        composed,
        node,
        sibling_node,
        kept2,
        kept2_other,
        kept3,
        kept3_other,
        near_field,
    )
    got3 = after(got3, lower)
    near_field = near_step(near_field, lower, [got3], [(0, 0, 6), (0, 64, 5)], 10**5)
    last = call(collect, shape(32, 5 * RANK), [VMEM] * 3 + [ANY], 10**8)(
        far_one, far_two, far_three, near_field
    )
    last_other = partner(last, 1)
    other3 = partner(
        call(second_half, shape(64, size), [VMEM, ANY], 10**5)(got3, last), 1
    )
    near_field = near_step(near_field, last, [other3], [(0, 0, -6)], 10**10)
    return call(finish, shape(32, size), [VMEM] * 8, 10**9)(
        codes, composed, near_field, lower, kept3, kept3_other, last, last_other
    )


def solution(mesh):
    placed = (
        P(None, "leaf"),
        P(None, "leaf"),
        P("leaf", None),
        P("leaf", None, None),
        P("leaf", None, None),
        P("leaf", None, None, None),
        P("leaf", None),
        P("leaf", None, None),
        P(),
    )
    return jax.shard_map(
        body, mesh=mesh, in_specs=placed, out_specs=P(None, "leaf"), check_vma=False
    )
```

```python
import functools
import math
import jax
import jax.numpy as jnp
from jax import lax
from jax.experimental import pallas as pl
from jax.experimental.pallas import tpu as pltpu
from jax.sharding import PartitionSpec as P

RANK = 256
LEVELS = 4
BLOCK = 256

f32 = jnp.float32
bf16 = jnp.bfloat16
SCALE = math.log2(math.e) / 16.0
NN = (((1,), (0,)), ((), ()))
NT = (((1,), (1,)), ((), ()))
VMEM = pl.BlockSpec(memory_space=pltpu.VMEM)
ANY = pl.BlockSpec(memory_space=pl.ANY)
HBM = pl.BlockSpec(memory_space=pltpu.HBM)


def mm(left, right, dims=NN):
    return lax.dot_general(left, right, dims, preferred_element_type=f32)


def split2(value):
    high = value.astype(bf16)
    return high, (value - high.astype(f32)).astype(bf16)


def split3(value):
    high = value.astype(bf16)
    rest = value - high.astype(f32)
    middle = rest.astype(bf16)
    return high, middle, (rest - middle.astype(f32)).astype(bf16)


def stack3(value):
    return jnp.concatenate(split3(value), axis=0)


def sum3(value):
    rows = value.shape[0] // 3
    return value[:rows] + value[rows : 2 * rows] + value[2 * rows :]


def norm_rows(value, first):
    count = value.shape[1]
    parts = split3(-SCALE * jnp.sum(value * value, axis=0, keepdims=True))
    parts = [part.astype(f32) for part in parts]
    ones = jnp.ones((3, count), f32)
    pad = jnp.zeros((10, count), f32)
    order = [*parts, ones, pad] if first else [ones, *parts, pad]
    return jnp.concatenate(order, axis=0).astype(bf16)


def own_features(points):
    a, b, c = split3(points * (2.0 * SCALE))
    return jnp.concatenate([a, a, b, b, a, c, norm_rows(points, True)], axis=0)


def other_features(points):
    a, b, c = split3(points)
    return jnp.concatenate([a, b, a, b, c, a, norm_rows(points, False)], axis=0)


def kernel_pieces(other, own):
    return split2(jnp.exp2(mm(other, own)))


def add_tile(other_points, other_charges, feature_ref, total_ref):
    other = other_features(other_points).T
    weights = stack3(other_charges)
    size = feature_ref.shape[1]
    for column in range(0, size, BLOCK):
        own = feature_ref[:, column : column + BLOCK]
        total = total_ref[:, column : column + BLOCK]
        for row in range(0, size, BLOCK):
            high, low = kernel_pieces(other[row : row + BLOCK], own)
            part = weights[:, row : row + BLOCK]
            total = total + mm(part, high) + mm(part, low)
        total_ref[:, column : column + BLOCK] = total


def pair(points, charges, other_points, other_charges, out):
    half = points.shape[0]
    for place, part in enumerate((points, charges, other_points, other_charges)):
        out[half * place : half * (place + 1)] = part[...]


def leaf_node(chip, chosen, matrix, out):
    size = chip.shape[1]
    spots = lax.broadcasted_iota(jnp.int32, (size, RANK), 0)
    marks = (spots == chosen[...]).astype(f32).astype(bf16)
    out[:32] = sum3(mm(stack3(chip[:32]), marks))
    high, low = split2(matrix[0])
    weights = stack3(chip[32:64])
    out[32:] = sum3(mm(weights, high, NT) + mm(weights, low, NT))


def near_first(near, chip, token, near_out, features, total):
    size = total.shape[1]
    me = lax.axis_index("leaf")
    features[...] = own_features(chip[:32])
    total[...] = jnp.zeros_like(total)
    add_tile(chip[:32], chip[32:64], features, total)
    sibling = me + 1 - 2 * lax.rem(me, 2)
    wanted = jnp.sum((near[...] == sibling).astype(jnp.int32))

    @pl.when(wanted > 0)
    def _():
        add_tile(chip[64:96], chip[96:], features, total)

    near_out[...] = sum3(total[...])


def near_blocks(entries, count, most, near, near_in, features, token, *refs):
    sources = refs[:count]
    near_out, slots, total, sems = refs[count:]
    me = lax.axis_index("leaf")
    sign = 2 * lax.rem(me, 2) - 1
    wanted = jnp.sum(lax.shift_left(jnp.int32(1), near[...] - me + 6))
    capped = most > 0 and not any(entry[3] for entry in entries)
    taken = jnp.int32(0)
    before = jnp.int32(0)
    for source, row, offset, kept_for_later in entries:
        bit = lax.rem(lax.shift_right_logical(wanted, sign * offset + 6), 2)
        if kept_for_later:
            before = before + bit
            bit = jnp.where(before > most, bit, 0)
        elif capped:
            bit = jnp.where(taken < most, bit, 0)

        @pl.when(bit == 1)
        def _(source=source, row=row, slot=taken):
            pltpu.make_async_copy(
                sources[source].at[pl.ds(row, 64)], slots.at[slot], sems.at[slot]
            ).start()

        taken = taken + bit
    total[...] = jnp.zeros_like(total)

    def step(slot, carry):
        pltpu.make_async_copy(
            sources[0].at[pl.ds(0, 64)], slots.at[slot], sems.at[slot]
        ).wait()
        add_tile(slots[slot, :32], slots[slot, 32:], features, total)
        return carry

    lax.fori_loop(0, taken, step, 0)
    near_out[...] = near_in[...] + sum3(total[...])


def block_of(ref, place):
    return ref[:, RANK * place : RANK * (place + 1)]


def merge(level, own, sibling, chosen, matrix, token, sent, *more):
    me = lax.axis_index("leaf")
    right = lax.rem(lax.shift_right_logical(me, level), 2)
    kind = lax.rem(me, 2)
    if level == 0:
        rows = pl.ds(pl.multiple_of(kind * 32, 32), 32)
        mine = own[rows, :]
        theirs = sibling[rows, :]
    else:
        mine = block_of(own, 2)
        theirs = block_of(sibling, 2)
        kept = more[-1]
        kept[:, : 2 * RANK] = sibling[:, : 2 * RANK]
        kept[:, 2 * RANK : 3 * RANK] = mine
        kept[:, 3 * RANK : 4 * RANK] = theirs
    sent[:, :RANK] = mine
    sent[:, RANK : 2 * RANK] = theirs
    mine = stack3(mine)
    theirs = stack3(theirs)
    first = right * RANK
    second = RANK - first

    @pl.when(kind == 0)
    def _():
        spots = lax.broadcasted_iota(jnp.int32, (RANK, RANK), 0)
        left_marks = (spots + first == chosen[level]).astype(f32).astype(bf16)
        right_marks = (spots + second == chosen[level]).astype(f32).astype(bf16)
        sent[:, 2 * RANK :] = sum3(mm(mine, left_marks) + mm(theirs, right_marks))

    @pl.when(kind == 1)
    def _():
        near_high, near_low = split2(
            matrix[0, level, :, pl.ds(pl.multiple_of(first, RANK), RANK)]
        )
        far_high, far_low = split2(
            matrix[0, level, :, pl.ds(pl.multiple_of(second, RANK), RANK)]
        )
        sent[:, 2 * RANK :] = sum3(
            (mm(mine, near_high, NT) + mm(mine, near_low, NT))
            + (mm(theirs, far_high, NT) + mm(theirs, far_low, NT))
        )

    if level == 2:
        more[0][...] = block_of(sent, 2)
        kept[:, 4 * RANK :] = block_of(sent, 2)


def collect(far_one, far_two, far_three, token, out):
    out[:, : 3 * RANK] = far_one[...]
    out[:, 3 * RANK : 4 * RANK] = far_two[...]
    out[:, 4 * RANK :] = far_three[...]


def sorted_kinds(pair, mine, theirs):
    kind = lax.rem(lax.axis_index("leaf"), 2)
    left = block_of(pair[0], mine)
    right = block_of(pair[1], theirs)
    return jnp.where(kind == 0, left, right), jnp.where(kind == 0, right, left)


def far_level(level, codes, own, choices):
    picked = []
    for position in range(2):
        code = codes[0, position : position + 1, level : level + 1]
        picked.append(
            [
                jnp.where(code == 1, one, jnp.where(code == 2, two, three))
                for one, two, three in zip(*choices, strict=True)
            ]
        )
    others = jnp.concatenate([picked[0][0], picked[1][0]], axis=1)
    weights = stack3(jnp.concatenate([picked[0][1], picked[1][1]], axis=1))
    high, low = kernel_pieces(other_features(others).T, own_features(own))
    return sum3(mm(weights, high) + mm(weights, low))


def product(left, right):
    high, low = split2(right)
    pieces = stack3(left)
    return sum3(mm(pieces, high) + mm(pieces, low))


def half_of(matrix, level):
    right = lax.rem(lax.shift_right_logical(lax.axis_index("leaf"), level), 2)
    return matrix[0, level, :, pl.ds(pl.multiple_of(right * RANK, RANK), RANK)]


def compose(upper_matrix, leaf_matrix, token, out):
    value = leaf_matrix[0]
    for level in range(3):
        value = product(half_of(upper_matrix, level), value)
        out[level] = value


def far_first(
    codes, gain, mine, leaf_matrix, composed, leaf_own, leaf_sibling, low, low_other, middle, middle_other, token, out
):
    low = (low, low_other)
    middle = (middle, middle_other)
    choices = [
        (leaf_sibling[:32], leaf_sibling[32:]),
        sorted_kinds(low, 0, 1),
        sorted_kinds(low, 1, 0),
    ]
    first = far_level(0, codes, leaf_own[:32], choices)
    choices = [sorted_kinds(low, 3, 3), sorted_kinds(middle, 0, 0), sorted_kinds(middle, 1, 1)]
    second = far_level(1, codes, sorted_kinds(low, 2, 2)[0], choices)
    count = gain.shape[1]
    diagonal = lax.broadcasted_iota(jnp.int32, (count, count), 0) == lax.broadcasted_iota(
        jnp.int32, (count, count), 1
    )
    column = jnp.sum(jnp.where(diagonal, gain[...], 0.0), axis=1, keepdims=True)
    far_out = product(first, leaf_matrix[0]) + product(second, composed[0])
    out[...] = far_out + column * mine[32:64]


def finish(codes, composed, near_field, lower, kept, kept_other, last, last_other, out):
    kept = (kept, kept_other)
    last = (last, last_other)
    choices = [sorted_kinds(kept, 3, 3), sorted_kinds(last, 0, 0), sorted_kinds(last, 1, 1)]
    third = far_level(2, codes, sorted_kinds(kept, 2, 2)[0], choices)
    choices = [sorted_kinds(last, place, place) for place in (2, 3, 4)]
    fourth = far_level(3, codes, sorted_kinds(kept, 4, 4)[0], choices)
    far_out = product(third, composed[1]) + product(fourth, composed[2])
    out[...] = (far_out + lower[...]) + near_field[...]


def call(function, shapes, in_specs, flops, scratch=(), limit=16, **extra):
    many = isinstance(shapes, list)
    return pl.pallas_call(
        function,
        out_shape=shapes,
        in_specs=in_specs,
        out_specs=[VMEM] * len(shapes) if many else VMEM,
        scratch_shapes=list(scratch),
        cost_estimate=pl.CostEstimate(flops=flops, bytes_accessed=1 << 20, transcendentals=0),
        compiler_params=pltpu.CompilerParams(vmem_limit_bytes=limit << 20),
        **extra,
    )


def gate(value, token, out):
    pass


def halve(value, token, whole, upper, lower):
    whole[...] = value[...]
    upper[...] = value[:64]
    lower[...] = value[64:]


def second_half(value, token, out):
    out[...] = value[64:]


def after(value, token):
    return pl.pallas_call(
        gate,
        out_shape=shape(*value.shape),
        in_specs=[ANY, ANY],
        out_specs=ANY,
        input_output_aliases={0: 0},
        compiler_params=pltpu.CompilerParams(vmem_limit_bytes=1 << 20),
    )(value, token)


def shape(rows, columns, kind=f32):
    return jax.ShapeDtypeStruct((rows, columns), kind)


def body(
    points,
    charges,
    leaf_skeleton,
    upper_skeleton,
    leaf_projection,
    upper_projection,
    near_leaves,
    far_codes,
    regularizer,
):
    devices = lax.axis_size("leaf")
    size = points.shape[1]

    def partner(value, bit):
        return lax.ppermute(value, "leaf", [(leaf, leaf ^ bit) for leaf in range(devices)])

    def along(value, chips):
        pairs = [(leaf, leaf + 2 * chips * (1 - 2 * (leaf % 2))) for leaf in range(devices)]
        pairs = [(source, target) for source, target in pairs if 0 <= target < devices]
        return lax.ppermute(value, "leaf", pairs)

    def near_step(near_field, token, sources, entries, flops, most=0):
        count = len(sources)
        return call(
            functools.partial(near_blocks, [(*entry, False)[:4] for entry in entries], count, most),
            shape(32, size),
            [VMEM] * 3 + [ANY] * (1 + count),
            flops,
            [
                pltpu.VMEM((len(entries), 64, size), f32),
                pltpu.VMEM((96, size), f32),
                pltpu.SemaphoreType.DMA((len(entries),)),
            ],
        )(near_leaves, near_field, features, token, *sources)

    def merge_step(level, own, sibling, token):
        shapes = [shape(32, 3 * RANK)]
        if level == 1:
            shapes += [shape(32, 4 * RANK)]
        if level == 2:
            shapes += [shape(32, RANK), shape(32, 5 * RANK)]
        return call(functools.partial(merge, level), shapes, [VMEM] * 4 + [ANY], 10**8)(
            own, sibling, upper_chosen, upper_projection, token
        )

    upper_chosen = jnp.transpose(upper_skeleton, (1, 0, 2))
    codes = jnp.transpose(far_codes, (0, 2, 1))

    chip = call(pair, shape(128, size), [VMEM] * 4, 10**8)(
        points, charges, partner(points, 1), partner(charges, 1)
    )
    got2 = along(chip, 2)
    got1 = along(chip, 1)
    node = call(leaf_node, shape(64, RANK), [VMEM] * 3, 10**11)(
        chip, leaf_skeleton, leaf_projection
    )
    sibling_node = partner(node, 1)
    (sent1,) = merge_step(0, node, sibling_node, node)
    far1 = partner(sent1, 2)
    near_field, features = call(
        near_first,
        [shape(32, size), shape(208, size, bf16)],
        [VMEM] * 2 + [ANY],
        2 * 10**9,
        [pltpu.VMEM((96, size), f32)],
    )(near_leaves, chip, sent1)
    composed = call(
        compose,
        jax.ShapeDtypeStruct((3, RANK, size), f32),
        [VMEM, VMEM, ANY],
        10**5,
    )(upper_projection, leaf_projection, near_field)
    got2, upper2, lower2 = call(
        halve, [shape(128, size), shape(64, size), shape(64, size)], [VMEM, ANY], 10**5
    )(got2, composed)
    sources = [got2, partner(upper2, 1), partner(lower2, 1)]
    entries = [(0, 0, 4), (0, 64, 3), (1, 0, -5), (2, 0, -4)]
    near_field = near_step(near_field, composed, sources, entries, 10**5, 3)
    sent2, kept2 = merge_step(1, sent1, far1, near_field)
    far2 = partner(sent2, 4)
    kept2_other = partner(kept2, 1)
    got1 = after(got1, sent2)
    got3 = along(got2, 1)
    other1 = partner(got1, 1)
    sent3, sent_few, kept3 = merge_step(2, sent2, far2, near_field)
    far_one = partner(sent3, 8)
    far_two = partner(sent_few, 16)
    far_three = partner(sent_few, 24)
    kept3_other = partner(kept3, 1)
    entries = [(0, 0, 2), (0, 64, 1), (1, 0, -3), (1, 64, -2)]
    entries += [(2, 0, 4, True), (2, 64, 3, True), (3, 0, -5, True), (4, 0, -4, True)]
    near_field = near_step(near_field, sent3, [got1, other1, *sources], entries, 4 * 10**10, 3)
    lower = call(far_first, shape(32, size), [VMEM] * 11 + [ANY], 10**8)(
        codes,
        regularizer[None, :],
        chip,
        leaf_projection,
        composed,
        node,
        sibling_node,
        kept2,
        kept2_other,
        kept3,
        kept3_other,
        near_field,
    )
    got3 = after(got3, lower)
    near_field = near_step(near_field, lower, [got3], [(0, 0, 6), (0, 64, 5)], 10**5)
    last = call(collect, shape(32, 5 * RANK), [VMEM] * 3 + [ANY], 10**8)(
        far_one, far_two, far_three, near_field
    )
    last_other = partner(last, 1)
    other3 = partner(
        call(second_half, shape(64, size), [VMEM, ANY], 10**5)(got3, last), 1
    )
    near_field = near_step(near_field, last, [other3], [(0, 0, -6)], 10**10)
    return call(finish, shape(32, size), [VMEM] * 8, 10**9)(
        codes, composed, near_field, lower, kept3, kept3_other, last, last_other
    )


def solution(mesh):
    placed = (
        P(None, "leaf"),
        P(None, "leaf"),
        P("leaf", None),
        P("leaf", None, None),
        P("leaf", None, None),
        P("leaf", None, None, None),
        P("leaf", None),
        P("leaf", None, None),
        P(),
    )
    return jax.shard_map(
        body, mesh=mesh, in_specs=placed, out_specs=P(None, "leaf"), check_vma=False
    )
```

```python
import functools
import math
import jax
import jax.numpy as jnp
from jax import lax
from jax.experimental import pallas as pl
from jax.experimental.pallas import tpu as pltpu
from jax.sharding import PartitionSpec as P

RANK = 256
LEVELS = 4
BLOCK = 256

f32 = jnp.float32
bf16 = jnp.bfloat16
SCALE = math.log2(math.e) / 16.0
NN = (((1,), (0,)), ((), ()))
NT = (((1,), (1,)), ((), ()))
VMEM = pl.BlockSpec(memory_space=pltpu.VMEM)
ANY = pl.BlockSpec(memory_space=pl.ANY)
HBM = pl.BlockSpec(memory_space=pltpu.HBM)


def mm(left, right, dims=NN):
    return lax.dot_general(left, right, dims, preferred_element_type=f32)


def split2(value):
    high = value.astype(bf16)
    return high, (value - high.astype(f32)).astype(bf16)


def split3(value):
    high = value.astype(bf16)
    rest = value - high.astype(f32)
    middle = rest.astype(bf16)
    return high, middle, (rest - middle.astype(f32)).astype(bf16)


def stack3(value):
    return jnp.concatenate(split3(value), axis=0)


def sum3(value):
    rows = value.shape[0] // 3
    return value[:rows] + value[rows : 2 * rows] + value[2 * rows :]


def norm_rows(value, first):
    count = value.shape[1]
    parts = split3(-SCALE * jnp.sum(value * value, axis=0, keepdims=True))
    parts = [part.astype(f32) for part in parts]
    ones = jnp.ones((3, count), f32)
    pad = jnp.zeros((10, count), f32)
    order = [*parts, ones, pad] if first else [ones, *parts, pad]
    return jnp.concatenate(order, axis=0).astype(bf16)


def own_features(points):
    a, b, c = split3(points * (2.0 * SCALE))
    return jnp.concatenate([a, a, b, b, a, c, norm_rows(points, True)], axis=0)


def other_features(points):
    a, b, c = split3(points)
    return jnp.concatenate([a, b, a, b, c, a, norm_rows(points, False)], axis=0)


def kernel_pieces(other, own):
    return split2(jnp.exp2(mm(other, own)))


def add_tile(other_points, other_charges, feature_ref, total_ref):
    other = other_features(other_points).T
    weights = stack3(other_charges)
    size = feature_ref.shape[1]
    for column in range(0, size, BLOCK):
        own = feature_ref[:, column : column + BLOCK]
        total = total_ref[:, column : column + BLOCK]
        for row in range(0, size, BLOCK):
            high, low = kernel_pieces(other[row : row + BLOCK], own)
            part = weights[:, row : row + BLOCK]
            total = total + mm(part, high) + mm(part, low)
        total_ref[:, column : column + BLOCK] = total


def pair(points, charges, other_points, other_charges, out):
    half = points.shape[0]
    for place, part in enumerate((points, charges, other_points, other_charges)):
        out[half * place : half * (place + 1)] = part[...]


def leaf_node(chip, chosen, matrix, out):
    size = chip.shape[1]
    spots = lax.broadcasted_iota(jnp.int32, (size, RANK), 0)
    marks = (spots == chosen[...]).astype(f32).astype(bf16)
    out[:32] = sum3(mm(stack3(chip[:32]), marks))
    high, low = split2(matrix[0])
    weights = stack3(chip[32:64])
    out[32:] = sum3(mm(weights, high, NT) + mm(weights, low, NT))


def near_first(near, chip, token, near_out, features, total):
    size = total.shape[1]
    me = lax.axis_index("leaf")
    features[...] = own_features(chip[:32])
    total[...] = jnp.zeros_like(total)
    add_tile(chip[:32], chip[32:64], features, total)
    sibling = me + 1 - 2 * lax.rem(me, 2)
    wanted = jnp.sum((near[...] == sibling).astype(jnp.int32))

    @pl.when(wanted > 0)
    def _():
        add_tile(chip[64:96], chip[96:], features, total)

    near_out[...] = sum3(total[...])


def near_blocks(entries, count, near, near_in, features, token, *refs):
    sources = refs[:count]
    near_out, slots, total, sems = refs[count:]
    me = lax.axis_index("leaf")
    sign = 2 * lax.rem(me, 2) - 1
    wanted = jnp.sum(lax.shift_left(jnp.int32(1), near[...] - me + 6))
    taken = jnp.int32(0)
    for source, row, offset in entries:
        bit = lax.rem(lax.shift_right_logical(wanted, sign * offset + 6), 2)

        @pl.when(bit == 1)
        def _(source=source, row=row, slot=taken):
            pltpu.make_async_copy(
                sources[source].at[pl.ds(row, 64)], slots.at[slot], sems.at[slot]
            ).start()

        taken = taken + bit
    total[...] = jnp.zeros_like(total)

    def step(slot, carry):
        pltpu.make_async_copy(
            sources[0].at[pl.ds(0, 64)], slots.at[slot], sems.at[slot]
        ).wait()
        add_tile(slots[slot, :32], slots[slot, 32:], features, total)
        return carry

    lax.fori_loop(0, taken, step, 0)
    near_out[...] = near_in[...] + sum3(total[...])


def block_of(ref, place):
    return ref[:, RANK * place : RANK * (place + 1)]


def merge(level, own, sibling, chosen, matrix, token, sent, *more):
    me = lax.axis_index("leaf")
    right = lax.rem(lax.shift_right_logical(me, level), 2)
    kind = lax.rem(me, 2)
    if level == 0:
        rows = pl.ds(pl.multiple_of(kind * 32, 32), 32)
        mine = own[rows, :]
        theirs = sibling[rows, :]
    else:
        mine = block_of(own, 2)
        theirs = block_of(sibling, 2)
        kept = more[-1]
        kept[:, : 2 * RANK] = sibling[:, : 2 * RANK]
        kept[:, 2 * RANK : 3 * RANK] = mine
        kept[:, 3 * RANK : 4 * RANK] = theirs
    sent[:, :RANK] = mine
    sent[:, RANK : 2 * RANK] = theirs
    mine = stack3(mine)
    theirs = stack3(theirs)
    first = right * RANK
    second = RANK - first

    @pl.when(kind == 0)
    def _():
        spots = lax.broadcasted_iota(jnp.int32, (RANK, RANK), 0)
        left_marks = (spots + first == chosen[level]).astype(f32).astype(bf16)
        right_marks = (spots + second == chosen[level]).astype(f32).astype(bf16)
        sent[:, 2 * RANK :] = sum3(mm(mine, left_marks) + mm(theirs, right_marks))

    @pl.when(kind == 1)
    def _():
        near_high, near_low = split2(
            matrix[0, level, :, pl.ds(pl.multiple_of(first, RANK), RANK)]
        )
        far_high, far_low = split2(
            matrix[0, level, :, pl.ds(pl.multiple_of(second, RANK), RANK)]
        )
        sent[:, 2 * RANK :] = sum3(
            (mm(mine, near_high, NT) + mm(mine, near_low, NT))
            + (mm(theirs, far_high, NT) + mm(theirs, far_low, NT))
        )

    if level == 2:
        more[0][...] = block_of(sent, 2)
        kept[:, 4 * RANK :] = block_of(sent, 2)


def collect(far_one, far_two, far_three, token, out):
    out[:, : 3 * RANK] = far_one[...]
    out[:, 3 * RANK : 4 * RANK] = far_two[...]
    out[:, 4 * RANK :] = far_three[...]


def sorted_kinds(pair, mine, theirs):
    kind = lax.rem(lax.axis_index("leaf"), 2)
    left = block_of(pair[0], mine)
    right = block_of(pair[1], theirs)
    return jnp.where(kind == 0, left, right), jnp.where(kind == 0, right, left)


def far_level(level, codes, own, choices):
    picked = []
    for position in range(2):
        code = codes[0, position : position + 1, level : level + 1]
        picked.append(
            [
                jnp.where(code == 1, one, jnp.where(code == 2, two, three))
                for one, two, three in zip(*choices, strict=True)
            ]
        )
    others = jnp.concatenate([picked[0][0], picked[1][0]], axis=1)
    weights = stack3(jnp.concatenate([picked[0][1], picked[1][1]], axis=1))
    high, low = kernel_pieces(other_features(others).T, own_features(own))
    return sum3(mm(weights, high) + mm(weights, low))


def product(left, right):
    high, low = split2(right)
    pieces = stack3(left)
    return sum3(mm(pieces, high) + mm(pieces, low))


def half_of(matrix, level):
    right = lax.rem(lax.shift_right_logical(lax.axis_index("leaf"), level), 2)
    return matrix[0, level, :, pl.ds(pl.multiple_of(right * RANK, RANK), RANK)]


def compose(upper_matrix, leaf_matrix, token, out):
    value = leaf_matrix[0]
    for level in range(3):
        value = product(half_of(upper_matrix, level), value)
        out[level] = value


def far_first(
    codes, gain, mine, leaf_matrix, composed, leaf_own, leaf_sibling, low, low_other, middle, middle_other, token, out
):
    low = (low, low_other)
    middle = (middle, middle_other)
    choices = [
        (leaf_sibling[:32], leaf_sibling[32:]),
        sorted_kinds(low, 0, 1),
        sorted_kinds(low, 1, 0),
    ]
    first = far_level(0, codes, leaf_own[:32], choices)
    choices = [sorted_kinds(low, 3, 3), sorted_kinds(middle, 0, 0), sorted_kinds(middle, 1, 1)]
    second = far_level(1, codes, sorted_kinds(low, 2, 2)[0], choices)
    count = gain.shape[1]
    diagonal = lax.broadcasted_iota(jnp.int32, (count, count), 0) == lax.broadcasted_iota(
        jnp.int32, (count, count), 1
    )
    column = jnp.sum(jnp.where(diagonal, gain[...], 0.0), axis=1, keepdims=True)
    far_out = product(first, leaf_matrix[0]) + product(second, composed[0])
    out[...] = far_out + column * mine[32:64]


def finish(codes, composed, near_field, lower, kept, kept_other, last, last_other, out):
    kept = (kept, kept_other)
    last = (last, last_other)
    choices = [sorted_kinds(kept, 3, 3), sorted_kinds(last, 0, 0), sorted_kinds(last, 1, 1)]
    third = far_level(2, codes, sorted_kinds(kept, 2, 2)[0], choices)
    choices = [sorted_kinds(last, place, place) for place in (2, 3, 4)]
    fourth = far_level(3, codes, sorted_kinds(kept, 4, 4)[0], choices)
    far_out = product(third, composed[1]) + product(fourth, composed[2])
    out[...] = (far_out + lower[...]) + near_field[...]


def call(function, shapes, in_specs, flops, scratch=(), limit=16, **extra):
    many = isinstance(shapes, list)
    return pl.pallas_call(
        function,
        out_shape=shapes,
        in_specs=in_specs,
        out_specs=[VMEM] * len(shapes) if many else VMEM,
        scratch_shapes=list(scratch),
        cost_estimate=pl.CostEstimate(flops=flops, bytes_accessed=1 << 20, transcendentals=0),
        compiler_params=pltpu.CompilerParams(vmem_limit_bytes=limit << 20),
        **extra,
    )


def gate(value, token, out):
    pass


def halve(value, token, whole, upper, lower):
    whole[...] = value[...]
    upper[...] = value[:64]
    lower[...] = value[64:]


def second_half(value, token, out):
    out[...] = value[64:]


def after(value, token):
    return pl.pallas_call(
        gate,
        out_shape=shape(*value.shape),
        in_specs=[ANY, ANY],
        out_specs=ANY,
        input_output_aliases={0: 0},
        compiler_params=pltpu.CompilerParams(vmem_limit_bytes=1 << 20),
    )(value, token)


def shape(rows, columns, kind=f32):
    return jax.ShapeDtypeStruct((rows, columns), kind)


def body(
    points,
    charges,
    leaf_skeleton,
    upper_skeleton,
    leaf_projection,
    upper_projection,
    near_leaves,
    far_codes,
    regularizer,
):
    devices = lax.axis_size("leaf")
    size = points.shape[1]

    def partner(value, bit):
        return lax.ppermute(value, "leaf", [(leaf, leaf ^ bit) for leaf in range(devices)])

    def along(value, chips):
        pairs = [(leaf, leaf + 2 * chips * (1 - 2 * (leaf % 2))) for leaf in range(devices)]
        pairs = [(source, target) for source, target in pairs if 0 <= target < devices]
        return lax.ppermute(value, "leaf", pairs)

    def near_step(near_field, token, sources, entries, flops):
        count = len(sources)
        return call(
            functools.partial(near_blocks, entries, count),
            shape(32, size),
            [VMEM] * 3 + [ANY] * (1 + count),
            flops,
            [
                pltpu.VMEM((len(entries), 64, size), f32),
                pltpu.VMEM((96, size), f32),
                pltpu.SemaphoreType.DMA((len(entries),)),
            ],
        )(near_leaves, near_field, features, token, *sources)

    def merge_step(level, own, sibling, token):
        shapes = [shape(32, 3 * RANK)]
        if level == 1:
            shapes += [shape(32, 4 * RANK)]
        if level == 2:
            shapes += [shape(32, RANK), shape(32, 5 * RANK)]
        return call(functools.partial(merge, level), shapes, [VMEM] * 4 + [ANY], 10**8)(
            own, sibling, upper_chosen, upper_projection, token
        )

    upper_chosen = jnp.transpose(upper_skeleton, (1, 0, 2))
    codes = jnp.transpose(far_codes, (0, 2, 1))

    chip = call(pair, shape(128, size), [VMEM] * 4, 10**8)(
        points, charges, partner(points, 1), partner(charges, 1)
    )
    got2 = along(chip, 2)
    got1 = along(chip, 1)
    node = call(leaf_node, shape(64, RANK), [VMEM] * 3, 10**11)(
        chip, leaf_skeleton, leaf_projection
    )
    sibling_node = partner(node, 1)
    (sent1,) = merge_step(0, node, sibling_node, node)
    far1 = partner(sent1, 2)
    near_field, features = call(
        near_first,
        [shape(32, size), shape(208, size, bf16)],
        [VMEM] * 2 + [ANY],
        2 * 10**9,
        [pltpu.VMEM((96, size), f32)],
    )(near_leaves, chip, sent1)
    composed = call(
        compose,
        jax.ShapeDtypeStruct((3, RANK, size), f32),
        [VMEM, VMEM, ANY],
        10**5,
    )(upper_projection, leaf_projection, near_field)
    got2, upper2, lower2 = call(
        halve, [shape(128, size), shape(64, size), shape(64, size)], [VMEM, ANY], 10**5
    )(got2, composed)
    sources = [got2, partner(upper2, 1), partner(lower2, 1)]
    entries = [(0, 0, 4), (0, 64, 3), (1, 0, -5), (2, 0, -4)]
    near_field = near_step(near_field, composed, sources, entries, 10**5)
    sent2, kept2 = merge_step(1, sent1, far1, near_field)
    far2 = partner(sent2, 4)
    kept2_other = partner(kept2, 1)
    got1 = after(got1, sent2)
    got3 = along(got2, 1)
    other1 = partner(got1, 1)
    sent3, sent_few, kept3 = merge_step(2, sent2, far2, near_field)
    far_one = partner(sent3, 8)
    far_two = partner(sent_few, 16)
    far_three = partner(sent_few, 24)
    kept3_other = partner(kept3, 1)
    entries = [(0, 0, 2), (0, 64, 1), (1, 0, -3), (1, 64, -2)]
    near_field = near_step(near_field, sent3, [got1, other1], entries, 4 * 10**10)
    lower = call(far_first, shape(32, size), [VMEM] * 11 + [ANY], 10**8)(
        codes,
        regularizer[None, :],
        chip,
        leaf_projection,
        composed,
        node,
        sibling_node,
        kept2,
        kept2_other,
        kept3,
        kept3_other,
        near_field,
    )
    got3 = after(got3, lower)
    near_field = near_step(near_field, lower, [got3], [(0, 0, 6), (0, 64, 5)], 10**5)
    last = call(collect, shape(32, 5 * RANK), [VMEM] * 3 + [ANY], 10**8)(
        far_one, far_two, far_three, near_field
    )
    last_other = partner(last, 1)
    other3 = partner(
        call(second_half, shape(64, size), [VMEM, ANY], 10**5)(got3, last), 1
    )
    near_field = near_step(near_field, last, [other3], [(0, 0, -6)], 10**10)
    return call(finish, shape(32, size), [VMEM] * 8, 10**9)(
        codes, composed, near_field, lower, kept3, kept3_other, last, last_other
    )


def solution(mesh):
    placed = (
        P(None, "leaf"),
        P(None, "leaf"),
        P("leaf", None),
        P("leaf", None, None),
        P("leaf", None, None),
        P("leaf", None, None, None),
        P("leaf", None),
        P("leaf", None, None),
        P(),
    )
    return jax.shard_map(
        body, mesh=mesh, in_specs=placed, out_specs=P(None, "leaf"), check_vma=False
    )
```

```python
import functools
import math
import jax
import jax.numpy as jnp
from jax import lax
from jax.experimental import pallas as pl
from jax.experimental.pallas import tpu as pltpu
from jax.sharding import PartitionSpec as P

RANK = 256
LEVELS = 4
BLOCK = 256

f32 = jnp.float32
bf16 = jnp.bfloat16
SCALE = math.log2(math.e) / 16.0
NN = (((1,), (0,)), ((), ()))
NT = (((1,), (1,)), ((), ()))
VMEM = pl.BlockSpec(memory_space=pltpu.VMEM)
ANY = pl.BlockSpec(memory_space=pl.ANY)
HBM = pl.BlockSpec(memory_space=pltpu.HBM)


def mm(left, right, dims=NN):
    return lax.dot_general(left, right, dims, preferred_element_type=f32)


def split2(value):
    high = value.astype(bf16)
    return high, (value - high.astype(f32)).astype(bf16)


def split3(value):
    high = value.astype(bf16)
    rest = value - high.astype(f32)
    middle = rest.astype(bf16)
    return high, middle, (rest - middle.astype(f32)).astype(bf16)


def stack3(value):
    return jnp.concatenate(split3(value), axis=0)


def sum3(value):
    rows = value.shape[0] // 3
    return value[:rows] + value[rows : 2 * rows] + value[2 * rows :]


def norm_rows(value, first):
    count = value.shape[1]
    parts = split3(-SCALE * jnp.sum(value * value, axis=0, keepdims=True))
    parts = [part.astype(f32) for part in parts]
    ones = jnp.ones((3, count), f32)
    pad = jnp.zeros((10, count), f32)
    order = [*parts, ones, pad] if first else [ones, *parts, pad]
    return jnp.concatenate(order, axis=0).astype(bf16)


def own_features(points):
    a, b, c = split3(points * (2.0 * SCALE))
    return jnp.concatenate([a, a, b, b, a, c, norm_rows(points, True)], axis=0)


def other_features(points):
    a, b, c = split3(points)
    return jnp.concatenate([a, b, a, b, c, a, norm_rows(points, False)], axis=0)


def kernel_pieces(other, own):
    return split2(jnp.exp2(mm(other, own)))


def add_tile(other_points, other_charges, feature_ref, total_ref):
    other = other_features(other_points).T
    weights = stack3(other_charges)
    size = feature_ref.shape[1]
    for column in range(0, size, BLOCK):
        own = feature_ref[:, column : column + BLOCK]
        total = total_ref[:, column : column + BLOCK]
        for row in range(0, size, BLOCK):
            high, low = kernel_pieces(other[row : row + BLOCK], own)
            part = weights[:, row : row + BLOCK]
            total = total + mm(part, high) + mm(part, low)
        total_ref[:, column : column + BLOCK] = total


def pair(points, charges, other_points, other_charges, out):
    half = points.shape[0]
    for place, part in enumerate((points, charges, other_points, other_charges)):
        out[half * place : half * (place + 1)] = part[...]


def leaf_node(chip, chosen, matrix, out):
    size = chip.shape[1]
    spots = lax.broadcasted_iota(jnp.int32, (size, RANK), 0)
    marks = (spots == chosen[...]).astype(f32).astype(bf16)
    out[:32] = sum3(mm(stack3(chip[:32]), marks))
    high, low = split2(matrix[0])
    weights = stack3(chip[32:64])
    out[32:] = sum3(mm(weights, high, NT) + mm(weights, low, NT))


def near_first(near, chip, token, near_out, features, total):
    size = total.shape[1]
    me = lax.axis_index("leaf")
    features[...] = own_features(chip[:32])
    total[...] = jnp.zeros_like(total)
    add_tile(chip[:32], chip[32:64], features, total)
    sibling = me + 1 - 2 * lax.rem(me, 2)
    wanted = jnp.sum((near[...] == sibling).astype(jnp.int32))

    @pl.when(wanted > 0)
    def _():
        add_tile(chip[64:96], chip[96:], features, total)

    near_out[...] = sum3(total[...])


def near_blocks(entries, count, near, near_in, features, token, *refs):
    sources = refs[:count]
    near_out, slots, total, sems = refs[count:]
    me = lax.axis_index("leaf")
    sign = 2 * lax.rem(me, 2) - 1
    wanted = jnp.sum(lax.shift_left(jnp.int32(1), near[...] - me + 6))
    taken = jnp.int32(0)
    for source, row, offset in entries:
        bit = lax.rem(lax.shift_right_logical(wanted, sign * offset + 6), 2)

        @pl.when(bit == 1)
        def _(source=source, row=row, slot=taken):
            pltpu.make_async_copy(
                sources[source].at[pl.ds(row, 64)], slots.at[slot], sems.at[slot]
            ).start()

        taken = taken + bit
    total[...] = jnp.zeros_like(total)

    def step(slot, carry):
        pltpu.make_async_copy(
            sources[0].at[pl.ds(0, 64)], slots.at[slot], sems.at[slot]
        ).wait()
        add_tile(slots[slot, :32], slots[slot, 32:], features, total)
        return carry

    lax.fori_loop(0, taken, step, 0)
    near_out[...] = near_in[...] + sum3(total[...])


def block_of(ref, place):
    return ref[:, RANK * place : RANK * (place + 1)]


def merge(level, own, sibling, chosen, matrix, token, sent, *more):
    me = lax.axis_index("leaf")
    right = lax.rem(lax.shift_right_logical(me, level), 2)
    kind = lax.rem(me, 2)
    if level == 0:
        rows = pl.ds(pl.multiple_of(kind * 32, 32), 32)
        mine = own[rows, :]
        theirs = sibling[rows, :]
    else:
        mine = block_of(own, 2)
        theirs = block_of(sibling, 2)
        kept = more[-1]
        kept[:, : 2 * RANK] = sibling[:, : 2 * RANK]
        kept[:, 2 * RANK : 3 * RANK] = mine
        kept[:, 3 * RANK : 4 * RANK] = theirs
    sent[:, :RANK] = mine
    sent[:, RANK : 2 * RANK] = theirs
    mine = stack3(mine)
    theirs = stack3(theirs)
    first = right * RANK
    second = RANK - first

    @pl.when(kind == 0)
    def _():
        spots = lax.broadcasted_iota(jnp.int32, (RANK, RANK), 0)
        left_marks = (spots + first == chosen[level]).astype(f32).astype(bf16)
        right_marks = (spots + second == chosen[level]).astype(f32).astype(bf16)
        sent[:, 2 * RANK :] = sum3(mm(mine, left_marks) + mm(theirs, right_marks))

    @pl.when(kind == 1)
    def _():
        near_high, near_low = split2(
            matrix[0, level, :, pl.ds(pl.multiple_of(first, RANK), RANK)]
        )
        far_high, far_low = split2(
            matrix[0, level, :, pl.ds(pl.multiple_of(second, RANK), RANK)]
        )
        sent[:, 2 * RANK :] = sum3(
            (mm(mine, near_high, NT) + mm(mine, near_low, NT))
            + (mm(theirs, far_high, NT) + mm(theirs, far_low, NT))
        )

    if level == 2:
        kept[:, 4 * RANK :] = block_of(sent, 2)


def couple(sent, far_one, token, out):
    out[:, :RANK] = block_of(sent, 2)
    out[:, RANK:] = block_of(far_one, 2)


def sorted_kinds(pair, mine, theirs):
    kind = lax.rem(lax.axis_index("leaf"), 2)
    left = block_of(pair[0], mine)
    right = block_of(pair[1], theirs)
    return jnp.where(kind == 0, left, right), jnp.where(kind == 0, right, left)


def far_level(level, codes, own, choices):
    picked = []
    for position in range(2):
        code = codes[0, position : position + 1, level : level + 1]
        picked.append(
            [
                jnp.where(code == 1, one, jnp.where(code == 2, two, three))
                for one, two, three in zip(*choices, strict=True)
            ]
        )
    others = jnp.concatenate([picked[0][0], picked[1][0]], axis=1)
    weights = stack3(jnp.concatenate([picked[0][1], picked[1][1]], axis=1))
    high, low = kernel_pieces(other_features(others).T, own_features(own))
    return sum3(mm(weights, high) + mm(weights, low))


def product(left, right):
    high, low = split2(right)
    pieces = stack3(left)
    return sum3(mm(pieces, high) + mm(pieces, low))


def half_of(matrix, level):
    right = lax.rem(lax.shift_right_logical(lax.axis_index("leaf"), level), 2)
    return matrix[0, level, :, pl.ds(pl.multiple_of(right * RANK, RANK), RANK)]


def compose(upper_matrix, leaf_matrix, token, out):
    value = leaf_matrix[0]
    for level in range(3):
        value = product(half_of(upper_matrix, level), value)
        out[level] = value


def far_first(
    codes, gain, mine, leaf_matrix, composed, leaf_own, leaf_sibling, low, low_other, middle, middle_other, token, out
):
    low = (low, low_other)
    middle = (middle, middle_other)
    choices = [
        (leaf_sibling[:32], leaf_sibling[32:]),
        sorted_kinds(low, 0, 1),
        sorted_kinds(low, 1, 0),
    ]
    first = far_level(0, codes, leaf_own[:32], choices)
    choices = [sorted_kinds(low, 3, 3), sorted_kinds(middle, 0, 0), sorted_kinds(middle, 1, 1)]
    second = far_level(1, codes, sorted_kinds(low, 2, 2)[0], choices)
    count = gain.shape[1]
    diagonal = lax.broadcasted_iota(jnp.int32, (count, count), 0) == lax.broadcasted_iota(
        jnp.int32, (count, count), 1
    )
    column = jnp.sum(jnp.where(diagonal, gain[...], 0.0), axis=1, keepdims=True)
    far_out = product(first, leaf_matrix[0]) + product(second, composed[0])
    out[...] = far_out + column * mine[32:64]


def far_second(codes, composed, lower, kept, kept_other, last, last_other, token, out):
    kept = (kept, kept_other)
    last = (last, last_other)
    choices = [sorted_kinds(kept, 3, 3), sorted_kinds(last, 0, 0), sorted_kinds(last, 1, 1)]
    field = far_level(2, codes, sorted_kinds(kept, 2, 2)[0], choices)
    out[...] = product(field, composed[1]) + lower[...]


def finish(codes, composed, near_field, lower, kept, kept_other, last, last_other, top, top_other, out):
    last = (last, last_other)
    top = (top, top_other)
    choices = [sorted_kinds(last, 2, 2), sorted_kinds(top, 0, 0), sorted_kinds(top, 1, 1)]
    field = far_level(3, codes, sorted_kinds((kept, kept_other), 4, 4)[0], choices)
    out[...] = (product(field, composed[2]) + lower[...]) + near_field[...]


def call(function, shapes, in_specs, flops, scratch=(), limit=16, **extra):
    many = isinstance(shapes, list)
    return pl.pallas_call(
        function,
        out_shape=shapes,
        in_specs=in_specs,
        out_specs=[VMEM] * len(shapes) if many else VMEM,
        scratch_shapes=list(scratch),
        cost_estimate=pl.CostEstimate(flops=flops, bytes_accessed=1 << 20, transcendentals=0),
        compiler_params=pltpu.CompilerParams(vmem_limit_bytes=limit << 20),
        **extra,
    )


def gate(value, token, out):
    pass


def halve(value, token, whole, upper, lower):
    whole[...] = value[...]
    upper[...] = value[:64]
    lower[...] = value[64:]


def second_half(value, token, out):
    out[...] = value[64:]


def after(value, token):
    return pl.pallas_call(
        gate,
        out_shape=shape(*value.shape),
        in_specs=[ANY, ANY],
        out_specs=ANY,
        input_output_aliases={0: 0},
        compiler_params=pltpu.CompilerParams(vmem_limit_bytes=1 << 20),
    )(value, token)


def shape(rows, columns, kind=f32):
    return jax.ShapeDtypeStruct((rows, columns), kind)


def body(
    points,
    charges,
    leaf_skeleton,
    upper_skeleton,
    leaf_projection,
    upper_projection,
    near_leaves,
    far_codes,
    regularizer,
):
    devices = lax.axis_size("leaf")
    size = points.shape[1]

    def partner(value, bit):
        return lax.ppermute(value, "leaf", [(leaf, leaf ^ bit) for leaf in range(devices)])

    def along(value, chips):
        pairs = [(leaf, leaf + 2 * chips * (1 - 2 * (leaf % 2))) for leaf in range(devices)]
        pairs = [(source, target) for source, target in pairs if 0 <= target < devices]
        return lax.ppermute(value, "leaf", pairs)

    def near_step(near_field, token, sources, entries, flops):
        count = len(sources)
        return call(
            functools.partial(near_blocks, entries, count),
            shape(32, size),
            [VMEM] * 3 + [ANY] * (1 + count),
            flops,
            [
                pltpu.VMEM((len(entries), 64, size), f32),
                pltpu.VMEM((96, size), f32),
                pltpu.SemaphoreType.DMA((len(entries),)),
            ],
        )(near_leaves, near_field, features, token, *sources)

    def merge_step(level, own, sibling, token):
        shapes = [shape(32, 3 * RANK)]
        if level == 1:
            shapes += [shape(32, 4 * RANK)]
        if level == 2:
            shapes += [shape(32, 5 * RANK)]
        return call(functools.partial(merge, level), shapes, [VMEM] * 4 + [ANY], 10**8)(
            own, sibling, upper_chosen, upper_projection, token
        )

    upper_chosen = jnp.transpose(upper_skeleton, (1, 0, 2))
    codes = jnp.transpose(far_codes, (0, 2, 1))

    chip = call(pair, shape(128, size), [VMEM] * 4, 10**8)(
        points, charges, partner(points, 1), partner(charges, 1)
    )
    got2 = along(chip, 2)
    got1 = along(chip, 1)
    node = call(leaf_node, shape(64, RANK), [VMEM] * 3, 10**11)(
        chip, leaf_skeleton, leaf_projection
    )
    sibling_node = partner(node, 1)
    (sent1,) = merge_step(0, node, sibling_node, node)
    far1 = partner(sent1, 2)
    near_field, features = call(
        near_first,
        [shape(32, size), shape(208, size, bf16)],
        [VMEM] * 2 + [ANY],
        2 * 10**9,
        [pltpu.VMEM((96, size), f32)],
    )(near_leaves, chip, sent1)
    composed = call(
        compose,
        jax.ShapeDtypeStruct((3, RANK, size), f32),
        [VMEM, VMEM, ANY],
        10**5,
    )(upper_projection, leaf_projection, near_field)
    got2, upper2, lower2 = call(
        halve, [shape(128, size), shape(64, size), shape(64, size)], [VMEM, ANY], 10**5
    )(got2, composed)
    sources = [got2, partner(upper2, 1), partner(lower2, 1)]
    entries = [(0, 0, 4), (0, 64, 3), (1, 0, -5), (2, 0, -4)]
    near_field = near_step(near_field, composed, sources, entries, 10**5)
    sent2, kept2 = merge_step(1, sent1, far1, near_field)
    far2 = partner(sent2, 4)
    kept2_other = partner(kept2, 1)
    got1 = after(got1, sent2)
    got3 = along(got2, 1)
    other1 = partner(got1, 1)
    sent3, kept3 = merge_step(2, sent2, far2, near_field)
    far_one = partner(sent3, 8)
    kept3_other = partner(kept3, 1)
    entries = [(0, 0, 2), (0, 64, 1), (1, 0, -3), (1, 64, -2)]
    near_field = near_step(near_field, sent3, [got1, other1], entries, 4 * 10**10)
    lower = call(far_first, shape(32, size), [VMEM] * 11 + [ANY], 10**8)(
        codes,
        regularizer[None, :],
        chip,
        leaf_projection,
        composed,
        node,
        sibling_node,
        kept2,
        kept2_other,
        kept3,
        kept3_other,
        near_field,
    )
    got3 = after(got3, lower)
    near_field = near_step(near_field, lower, [got3], [(0, 0, 6), (0, 64, 5)], 10**5)
    sent4 = call(couple, shape(32, 2 * RANK), [VMEM] * 2 + [ANY], 10**5)(
        sent3, far_one, near_field
    )
    far_top = partner(sent4, 16)
    far_one = after(far_one, sent4)
    far_one_other = partner(far_one, 1)
    other3 = partner(
        call(second_half, shape(64, size), [VMEM, ANY], 10**5)(got3, sent4), 1
    )
    near_field = near_step(near_field, sent4, [other3], [(0, 0, -6)], 10**5)
    lower = call(far_second, shape(32, size), [VMEM] * 7 + [ANY], 10**10)(
        codes, composed, lower, kept3, kept3_other, far_one, far_one_other, near_field
    )
    far_top = after(far_top, lower)
    far_top_other = partner(far_top, 1)
    return call(finish, shape(32, size), [VMEM] * 10, 10**9)(
        codes,
        composed,
        near_field,
        lower,
        kept3,
        kept3_other,
        far_one,
        far_one_other,
        far_top,
        far_top_other,
    )


def solution(mesh):
    placed = (
        P(None, "leaf"),
        P(None, "leaf"),
        P("leaf", None),
        P("leaf", None, None),
        P("leaf", None, None),
        P("leaf", None, None, None),
        P("leaf", None),
        P("leaf", None, None),
        P(),
    )
    return jax.shard_map(
        body, mesh=mesh, in_specs=placed, out_specs=P(None, "leaf"), check_vma=False
    )
```
